32 devices in a mesh: groups: 2 (over y), ctx: 4 (over z), tp: 2 (over x), rep: 2 (over core).
Axes of the slice: x: 2, y: 2, z: 4, core: 2. Of those that a mesh axis runs over, the one named last changes fastest.
Arguments:
- queries: bfloat16 [4096, 32, 128], P(('groups', 'ctx'), ('tp', 'rep')), parts along dimension 0, may hold values from -64 to 64
- keys: bfloat16 [4096, 8, 128], P(('groups', 'ctx'), 'tp'), parts along dimension 0, may hold values from -13 to 13
- values: bfloat16 [4096, 8, 128], P(('groups', 'ctx'), 'tp'), parts along dimension 0, may hold values from -6 to 6
- lengths: int32 [8], P('groups'), parts along dimension 0, may hold values from 1 to 1024, 2048 in all
- page_ranks: int32 [32], P(('groups', 'ctx')), parts along dimension 0, may hold values from 0 to 3, as said below
Outputs:
- context: bfloat16 [4096, 32, 128], P(('groups', 'ctx'), ('tp', 'rep')), parts along dimension 0
- decode_cache: bfloat16 [8, 4, 128, 2, 8, 128], P(('groups', 'ctx'), None, None, 'rep', 'tp'), parts along dimension 0
The draws below stay inside these ranges and needn't reach their ends.
There are 2 independent parts, one for each index of `groups`. The reference program is written for one: setup_inputs(seed, part) draws one part's arguments, and reference() takes and returns one part's arrays. A program takes and returns all parts, laid end to end along the dimension named above; each array names one. Nothing has to cross between parts.
Inputs may be any that keep to these rules, and one draw needn't show every extreme that they name: `page_ranks`: pages 4 * s to 4 * s + 3 go to distinct decode ranks, for every s; one decode rank receives a page from every s.
All inputs are finite; a program needn't handle non-finite values.
Results may differ from the reference program's by a relative error of at most 0.0037.
Values may be sent and summed in bfloat16 or wider, within the bound.
A program may use at most 128 MiB of HBM per device.

```python
import math
import jax
import jax.numpy as jnp
import numpy as np
from jax import lax

QH = 32
KVH = 8
HD = 128
PAGE = 128
NREQ = 4
SEQ = 2048
PAGES_DEV = 4
PAGES = 16
N_CTX = 4


def shared_keys(key):
    base = jnp.clip(jax.random.normal(jax.random.fold_in(key, 101), (SEQ, KVH, HD), jnp.float32), -5.0, 5.0)
    return base


def draw_keys(key, part):
    base = shared_keys(key)
    return base.astype(jnp.bfloat16)


def draw_queries(key, part):
    key = jax.random.fold_in(key, 2)
    own = jnp.clip(jax.random.normal(key, (SEQ, QH, HD), jnp.float32), -5.0, 5.0)
    return own.astype(jnp.bfloat16)


def draw_page_ranks(key, part):
    key = jax.random.fold_in(key, 3)
    hottest = jax.random.randint(jax.random.fold_in(key, 1), (), 0, N_CTX)
    ranks = jnp.arange(N_CTX, dtype=jnp.int32)

    def one_source(subkey):
        scores = jax.random.randint(subkey, (N_CTX,), 0, 2 ** 20) * N_CTX + ranks
        scores = scores + jnp.where(ranks == hottest, 2 ** 26, 0)
        picked = lax.top_k(scores, PAGES_DEV)[1]
        return jax.random.permutation(jax.random.fold_in(subkey, 7), picked)
    subkeys = jax.random.split(jax.random.fold_in(key, 2), N_CTX)
    return jax.vmap(one_source)(subkeys).reshape(-1).astype(jnp.int32)


def levels(rng, dims, pieces, smallest, high):
    def one(position, shards_of):
        draws = jax.random.uniform(jax.random.fold_in(jax.random.fold_in(rng, 6), position), (shards_of,), jnp.float32, smallest / len(pieces), high / len(pieces))
        return jnp.repeat(jnp.exp(draws), dims[position] // shards_of).reshape((-1,) + (1,) * (len(dims) - position - 1))

    factor_of = one(*pieces[0])
    for cut in pieces[1:]:
        factor_of = factor_of * one(*cut)
    return factor_of


def split_up(number_of, total, most, skew):
    portions = [(1 << 20) // math.isqrt(standing ** skew) + 1 for standing in range(2, number_of + 1)]
    spare, given = total - most - (number_of - 1), [1] * (number_of - 1)
    while spare > 0:
        movable = [i for i in range(number_of - 1) if given[i] < most]
        mass, left = sum([portions[i] for i in movable]), spare
        for i in movable:
            addition = min(most - given[i], max(1, left * portions[i] // mass), spare)
            given[i] = given[i] + addition
            spare = spare - addition
    return np.array([most] + given)


def uneven_parts(own_key, count, total, limit, lean):
    if count == 2:
        one = jax.random.randint(own_key, (), max(1, total - limit), min(limit, total - 1) + 1)
        return jnp.stack([one, total - one])
    sizes = jnp.asarray(split_up(count, total, limit, lean), jnp.int32)
    couples = (count - 1) // 2
    source_of, sink = sizes[1:1 + 2 * couples:2], sizes[2:2 + 2 * couples:2]
    slack = jnp.minimum(source_of - 1, limit - sink)
    moved = jax.random.randint(jax.random.fold_in(own_key, 1), (couples,), 0, 1 << 20) % (slack + 1)
    sizes = sizes.at[1:1 + 2 * couples:2].set(source_of - moved).at[2:2 + 2 * couples:2].set(sink + moved)
    return sizes[jax.random.permutation(jax.random.fold_in(own_key, 2), count)]


def gaussian(rng, extent, spread, most, cuts=(), kind=jnp.bfloat16):
    drawn = jax.random.normal(rng, extent, jnp.float32) * spread
    if len(cuts) > 0:
        drawn = levels(rng, extent, cuts, -0.22, 0.18) * drawn
    return jnp.clip(drawn, min=-most, max=most).astype(kind)


def setup_inputs(seed: int = 0, part: int = 0) -> dict:
    arg_keys = jax.random.split(jax.random.key(seed), 6)
    part_keys = jax.random.split(jax.random.fold_in(arg_keys[5], part), 6)
    queries = draw_queries(jax.random.fold_in(jax.random.fold_in(arg_keys[5], part), 71), part)
    keys = draw_keys(jax.random.fold_in(jax.random.fold_in(arg_keys[5], part), 71), part)
    values = gaussian(part_keys[2], (SEQ, KVH, HD), 1.0, 6.0, ((0, 4), (1, 2)))
    lengths = uneven_parts(part_keys[3], NREQ, SEQ, SEQ // 2, 2).astype(jnp.int32)
    page_ranks = draw_page_ranks(jax.random.fold_in(jax.random.fold_in(arg_keys[5], part), 71), part)
    return dict(queries=queries, keys=keys, values=values, lengths=lengths, page_ranks=page_ranks)


neg_fill = -1.0e30


def reference(queries, keys, values, lengths, page_ranks):
    ends = jnp.cumsum(lengths).astype(jnp.int32)
    positions = jnp.arange(SEQ, dtype=jnp.int32)
    segment = jnp.sum((positions[:, None] >= ends[None, :]).astype(jnp.int32), axis=1)
    allowed = (segment[:, None] == segment[None, :]) & (positions[None, :] <= positions[:, None])
    group = QH // KVH
    scale = HD ** -0.5

    def one_head(head):
        query = lax.dynamic_index_in_dim(queries, head, 1, False)
        key = lax.dynamic_index_in_dim(keys, head // group, 1, False)
        value = lax.dynamic_index_in_dim(values, head // group, 1, False)
        score = jnp.dot(query, key.T, preferred_element_type=jnp.float32) * scale
        score = jnp.where(allowed, score, neg_fill)
        peak = jnp.max(score, axis=1, keepdims=True)
        weight = jnp.where(allowed, jnp.exp(score - peak), 0.0)
        total = jnp.sum(weight, axis=1, keepdims=True)
        mixed = jnp.dot(weight.astype(jnp.bfloat16), value, preferred_element_type=jnp.float32) / total
        return mixed.astype(jnp.bfloat16)

    context = jnp.transpose(lax.map(one_head, jnp.arange(QH, dtype=jnp.int32)), (1, 0, 2))
    key_pages = keys.reshape(PAGES, PAGE, KVH, HD)
    value_pages = values.reshape(PAGES, PAGE, KVH, HD)
    stacked = jnp.stack([key_pages, value_pages], axis=2)
    source = jnp.arange(PAGES, dtype=jnp.int32) // PAGES_DEV
    decode_cache = jnp.zeros((N_CTX, N_CTX, PAGE, 2, KVH, HD), jnp.bfloat16).at[page_ranks, source].set(stacked)
    return context, decode_cache
```

```python
import functools
import math

import jax
import jax.numpy as jnp
from jax import lax
from jax.experimental import pallas as pl
from jax.experimental.pallas import tpu as pltpu
from jax.sharding import PartitionSpec as P

PAGE = 128
MESH = pl.DeviceIdType.MESH
NEG = -1e30


def wide(x, lanes):
    return jnp.concatenate([x] * (lanes // 128), axis=1) if lanes > 128 else x


def kernel(
    n, window, heads, group, lengths, ranks, q_ref, kv_ref, out_ref, dec_ref,
    buf, mask_tx, mask_rx, stage, start_ref, acc, peak, total,
    z_send, z_recv, c_send, c_recv, m_send, m_recv, p_send, p_recv,
):
    me = lax.axis_index("ctx")
    core = lax.axis_index("rep")
    tok, kvw = kv_ref.shape[1:]
    half = tok // 2
    pages = tok // PAGE
    factor = 128 ** -0.5 * math.log2(math.e)

    barrier = pltpu.get_barrier_semaphore()
    for step in range(1, n):
        pl.semaphore_signal(
            barrier, inc=1, device_id={"ctx": lax.rem(me + step, n)}, device_id_type=MESH
        )
    pl.semaphore_signal(barrier, inc=1, device_id={"rep": 1 - core}, device_id_type=MESH)
    pl.semaphore_wait(barrier, n)

    def rows(part):
        return pl.ds(part * half, half)

    def block_copy(d, part):
        return pltpu.make_async_remote_copy(
            src_ref=kv_ref.at[core, rows(part)],
            dst_ref=buf.at[core, d - 1, rows(part)],
            send_sem=z_send.at[d - 1, part],
            recv_sem=z_recv.at[d - 1, part],
            device_id={"ctx": lax.rem(me + d, n)},
            device_id_type=MESH,
        )

    def core_copy(d, part, which):
        return pltpu.make_async_remote_copy(
            src_ref=buf.at[which, d - 1, rows(part)],
            dst_ref=buf.at[which, d - 1, rows(part)],
            send_sem=c_send.at[d - 1, part],
            recv_sem=c_recv.at[d - 1, part],
            device_id={"rep": 1 - core},
            device_id_type=MESH,
        )

    def mask_copy(d):
        return pltpu.make_async_remote_copy(
            src_ref=mask_tx.at[d - 1],
            dst_ref=mask_rx.at[d - 1],
            send_sem=m_send.at[d - 1],
            recv_sem=m_recv.at[d - 1],
            device_id={"ctx": lax.rem(me + d, n)},
            device_id_type=MESH,
        )

    def page_copy(there, slot):
        return pltpu.make_async_remote_copy(
            src_ref=stage.at[there],
            dst_ref=dec_ref.at[slot],
            send_sem=p_send.at[there],
            recv_sem=p_recv.at[slot],
            device_id={"ctx": there},
            device_id_type=MESH,
        )

    def page_for(rank):
        page = jnp.zeros((PAGE, kvw), jnp.bfloat16)
        for g in range(pages):
            flag = jnp.where(ranks[g] == rank, jnp.float32(1), jnp.float32(0))
            flag = jnp.full((PAGE, kvw), flag, jnp.float32).astype(jnp.bfloat16)
            page = page + flag * kv_ref[core, pl.ds(g * PAGE, PAGE), :]
        return page

    def start_blocks(d):
        @pl.when(me + d < n)
        def _():
            for part in (1, 0):
                block_copy(d, part).start()

    start_blocks(1)
    mask_tx[...] = jnp.zeros_like(mask_tx)

    for there in range(n):
        @pl.when((there < me) | (there > me + window))
        def _(there=there):
            stage[there] = page_for(there)
            page_copy(there, me).start()

    for d in range(1, window + 1):
        @pl.when(me + d < n)
        def _(d=d):
            for g in range(pages):
                chosen = jnp.where(ranks[g] == me + d, jnp.float32(1), jnp.float32(0))
                mask_tx[d - 1, g : g + 1, :] = jnp.full((1, 128), chosen, jnp.float32)
            mask_copy(d).start()

    dec_ref[me] = page_for(me)

    pos = me * tok + lax.broadcasted_iota(jnp.int32, (tok, 128), 0)
    first = jnp.zeros((tok, 128), jnp.int32)
    end = jnp.int32(0)
    for r in range(lengths.shape[0]):
        end = end + lengths[r]
        first = jnp.where(pos >= end, end, first)
    start_ref[...] = first

    def attend(keys_at, values_at, base, k0, kn, q0, qn, own):
        def one(h, carry):
            lane = pl.ds(pl.multiple_of(((core * heads + h) // group) * 128, 128), 128)
            mine = pl.ds(pl.multiple_of(h * 128, 128), 128)
            k = keys_at[pl.ds(k0, kn), lane]
            v = values_at[pl.ds(k0, kn), lane]
            score = lax.dot_general(
                q_ref[pl.ds(q0, qn), mine], k, (((1,), (1,)), ((), ())),
                preferred_element_type=jnp.float32,
            )
            key_pos = base + k0 + lax.broadcasted_iota(jnp.int32, (qn, kn), 1)
            allowed = key_pos >= wide(start_ref[pl.ds(q0, qn), :], kn)
            if own:
                query_pos = base + q0 + lax.broadcasted_iota(jnp.int32, (qn, kn), 0)
                allowed = allowed & (key_pos <= query_pos)
            score = jnp.where(allowed, score, NEG)
            top = jnp.broadcast_to(jnp.max(score, axis=1, keepdims=True), (qn, 128))
            span = pl.ds(q0, qn)
            if not own:
                old = peak[h, span, :]
                top = jnp.maximum(old, top)
            weight = jnp.exp2((score - wide(top, kn)) * factor)
            part = weight[:, :128]
            for c in range(128, kn, 128):
                part = part + weight[:, c : c + 128]
            mixed = jnp.dot(weight.astype(jnp.bfloat16), v, preferred_element_type=jnp.float32)
            if not own:
                keep = jnp.exp2((old - top) * factor)
                part = part + keep * total[h, span, :]
                mixed = mixed + keep * acc[h, span, :]
            peak[h, span, :] = top
            total[h, span, :] = part
            acc[h, span, :] = mixed
            return carry

        lax.fori_loop(0, heads, one, 0, unroll=2)

    mine_k, mine_v = kv_ref.at[0], kv_ref.at[1]
    attend(mine_k, mine_v, me * tok, 0, half, 0, half, True)
    attend(mine_k, mine_v, me * tok, 0, tok, half, half, True)

    for d in range(1, window + 1):
        @pl.when(me + d < n)
        def _(d=d):
            for part in (1, 0):
                block_copy(d, part).wait_send()

        if d < window:
            start_blocks(d + 1)

        @pl.when(me >= d)
        def _(d=d):
            base = (me - d) * tok
            for part in (1, 0):
                block_copy(d, part).wait_recv()
                core_copy(d, part, core).start()
                core_copy(d, part, 1 - core).wait_recv()
                shorter = d == window and part == 0 and 2 * window == n
                attend(
                    buf.at[0, d - 1], buf.at[1, d - 1], base, part * half, half,
                    0, half if shorter else tok, False,
                )
            mask_copy(d).wait_recv()
            chosen = jnp.zeros((PAGE, kvw), jnp.bfloat16)
            for g in range(pages):
                flag = jnp.broadcast_to(mask_rx[d - 1, g : g + 1, :], (PAGE, 128))
                chosen = chosen + wide(flag.astype(jnp.bfloat16), kvw) * buf[
                    core, d - 1, pl.ds(g * PAGE, PAGE), :
                ]
            dec_ref[me - d] = chosen
            for part in (1, 0):
                core_copy(d, part, core).wait_send()

    def finish(h, carry):
        mine = pl.ds(pl.multiple_of(h * 128, 128), 128)
        whole = jnp.sum(total[h], axis=1, keepdims=True)
        out_ref[:, mine] = (acc[h] / whole).astype(jnp.bfloat16)
        return carry

    lax.fori_loop(0, heads, finish, 0)

    for d in range(1, window + 1):
        @pl.when(me + d < n)
        def _(d=d):
            mask_copy(d).wait_send()

    for other in range(n):
        @pl.when((other < me) | (other > me + window))
        def _(other=other):
            page_copy(other, me).wait_send()

        @pl.when((other > me) | (other < me - window))
        def _(other=other):
            page_copy(other, other).wait_recv()


def body(queries, keys, values, lengths, page_ranks):
    tok, heads, dim = queries.shape
    kv_heads = keys.shape[1]
    n = lax.axis_size("ctx")
    rep = lax.axis_size("rep")
    window = n // 2
    group = heads * rep // kv_heads
    kvw = kv_heads * dim
    kv = jnp.stack([keys.reshape(tok, kvw), values.reshape(tok, kvw)])
    vmem = pl.BlockSpec(memory_space=pltpu.VMEM)
    smem = pl.BlockSpec(memory_space=pltpu.SMEM)
    flag_rows = -(-(tok // PAGE) // 8) * 8
    dma = pltpu.SemaphoreType.DMA
    context, cache = pl.pallas_call(
        functools.partial(kernel, n, window, heads, group),
        out_shape=(
            jax.ShapeDtypeStruct((tok, heads * dim), jnp.bfloat16),
            jax.ShapeDtypeStruct((n, PAGE, kvw), jnp.bfloat16),
        ),
        in_specs=[smem, smem, vmem, vmem],
        out_specs=(vmem, vmem),
        scratch_shapes=[
            pltpu.VMEM((2, window, tok, kvw), jnp.bfloat16),
            pltpu.VMEM((window, flag_rows, 128), jnp.float32),
            pltpu.VMEM((window, flag_rows, 128), jnp.float32),
            pltpu.VMEM((n, PAGE, kvw), jnp.bfloat16),
            pltpu.VMEM((tok, 128), jnp.int32),
            pltpu.VMEM((heads, tok, 128), jnp.float32),
            pltpu.VMEM((heads, tok, 128), jnp.float32),
            pltpu.VMEM((heads, tok, 128), jnp.float32),
            dma((window, 2)),
            dma((window, 2)),
            dma((window, 2)),
            dma((window, 2)),
            dma((window,)),
            dma((window,)),
            dma((n,)),
            dma((n,)),
        ],
        compiler_params=pltpu.CompilerParams(
            collective_id=0, has_side_effects=True, vmem_limit_bytes=48 * 1024 * 1024
        ),
        cost_estimate=pl.CostEstimate(
            flops=4 * heads * tok * tok * 2 * dim, bytes_accessed=8 * tok * kvw,
            transcendentals=heads * tok * tok * 2,
        ),
    )(lengths, page_ranks, queries.reshape(tok, heads * dim), kv)
    return (
        context.reshape(tok, heads, dim),
        cache.reshape(1, n, PAGE, 1, kv_heads, dim),
    )


def solution(mesh):
    in_specs = (
        P(("groups", "ctx"), ("tp", "rep"), None),
        P(("groups", "ctx"), "tp", None),
        P(("groups", "ctx"), "tp", None),
        P("groups"),
        P(("groups", "ctx")),
    )
    out_specs = (
        P(("groups", "ctx"), ("tp", "rep"), None),
        P(("groups", "ctx"), None, None, "rep", "tp", None),
    )
    return jax.shard_map(body, mesh=mesh, in_specs=in_specs, out_specs=out_specs, check_vma=False)
```

```python
import functools
import math

import jax
import jax.numpy as jnp
from jax import lax
from jax.experimental import pallas as pl
from jax.experimental.pallas import tpu as pltpu
from jax.sharding import PartitionSpec as P

PAGE = 128
MESH = pl.DeviceIdType.MESH
NEG = -1e30


def wide(x, lanes):
    return jnp.concatenate([x] * (lanes // 128), axis=1) if lanes > 128 else x


def kernel(
    n, window, heads, group, lengths, ranks, q_ref, kv_ref, out_ref, dec_ref,
    buf, mask_tx, mask_rx, stage, start_ref, acc, peak, total,
    z_send, z_recv, c_send, c_recv, m_send, m_recv, p_send, p_recv,
):
    me = lax.axis_index("ctx")
    core = lax.axis_index("rep")
    tok, kvw = kv_ref.shape[1:]
    half = tok // 2
    pages = tok // PAGE
    factor = 128 ** -0.5 * math.log2(math.e)

    barrier = pltpu.get_barrier_semaphore()
    for step in range(1, n):
        pl.semaphore_signal(
            barrier, inc=1, device_id={"ctx": lax.rem(me + step, n)}, device_id_type=MESH
        )
    pl.semaphore_signal(barrier, inc=1, device_id={"rep": 1 - core}, device_id_type=MESH)
    pl.semaphore_wait(barrier, n)

    def rows(part):
        return pl.ds(part * half, half)

    def block_copy(d, part):
        own = kv_ref.at[core, rows(part)]
        return pltpu.make_async_remote_copy(
            src_ref=own if d == 1 else buf.at[core, d - 2, rows(part)],
            dst_ref=buf.at[core, d - 1, rows(part)],
            send_sem=z_send.at[d - 1, part],
            recv_sem=z_recv.at[d - 1, part],
            device_id={"ctx": lax.rem(me + 1, n)},
            device_id_type=MESH,
        )

    def core_copy(d, part, which):
        return pltpu.make_async_remote_copy(
            src_ref=buf.at[which, d - 1, rows(part)],
            dst_ref=buf.at[which, d - 1, rows(part)],
            send_sem=c_send.at[d - 1, part],
            recv_sem=c_recv.at[d - 1, part],
            device_id={"rep": 1 - core},
            device_id_type=MESH,
        )

    def mask_copy(d):
        return pltpu.make_async_remote_copy(
            src_ref=mask_tx.at[d - 1],
            dst_ref=mask_rx.at[d - 1],
            send_sem=m_send.at[d - 1],
            recv_sem=m_recv.at[d - 1],
            device_id={"ctx": lax.rem(me + d, n)},
            device_id_type=MESH,
        )

    def page_copy(there, slot):
        return pltpu.make_async_remote_copy(
            src_ref=stage.at[there],
            dst_ref=dec_ref.at[slot],
            send_sem=p_send.at[there],
            recv_sem=p_recv.at[slot],
            device_id={"ctx": there},
            device_id_type=MESH,
        )

    def page_for(rank):
        page = jnp.zeros((PAGE, kvw), jnp.bfloat16)
        for g in range(pages):
            flag = jnp.where(ranks[g] == rank, jnp.float32(1), jnp.float32(0))
            flag = jnp.full((PAGE, kvw), flag, jnp.float32).astype(jnp.bfloat16)
            page = page + flag * kv_ref[core, pl.ds(g * PAGE, PAGE), :]
        return page

    @pl.when(me + 1 < n)
    def _():
        for part in (1, 0):
            block_copy(1, part).start()

    mask_tx[...] = jnp.zeros_like(mask_tx)

    for there in range(n):
        @pl.when((there < me) | (there > me + window))
        def _(there=there):
            stage[there] = page_for(there)
            page_copy(there, me).start()

    for d in range(1, window + 1):
        @pl.when(me + d < n)
        def _(d=d):
            for g in range(pages):
                chosen = jnp.where(ranks[g] == me + d, jnp.float32(1), jnp.float32(0))
                mask_tx[d - 1, g : g + 1, :] = jnp.full((1, 128), chosen, jnp.float32)
            mask_copy(d).start()

    dec_ref[me] = page_for(me)

    pos = me * tok + lax.broadcasted_iota(jnp.int32, (tok, 128), 0)
    first = jnp.zeros((tok, 128), jnp.int32)
    end = jnp.int32(0)
    for r in range(lengths.shape[0]):
        end = end + lengths[r]
        first = jnp.where(pos >= end, end, first)
    start_ref[...] = first

    def attend(keys_at, values_at, base, k0, kn, q0, qn, own):
        def one(h, carry):
            lane = pl.ds(pl.multiple_of(((core * heads + h) // group) * 128, 128), 128)
            mine = pl.ds(pl.multiple_of(h * 128, 128), 128)
            k = keys_at[pl.ds(k0, kn), lane]
            v = values_at[pl.ds(k0, kn), lane]
            score = lax.dot_general(
                q_ref[pl.ds(q0, qn), mine], k, (((1,), (1,)), ((), ())),
                preferred_element_type=jnp.float32,
            )
            key_pos = base + k0 + lax.broadcasted_iota(jnp.int32, (qn, kn), 1)
            allowed = key_pos >= wide(start_ref[pl.ds(q0, qn), :], kn)
            if own:
                query_pos = base + q0 + lax.broadcasted_iota(jnp.int32, (qn, kn), 0)
                allowed = allowed & (key_pos <= query_pos)
            score = jnp.where(allowed, score, NEG)
            top = jnp.broadcast_to(jnp.max(score, axis=1, keepdims=True), (qn, 128))
            span = pl.ds(q0, qn)
            if not own:
                old = peak[h, span, :]
                top = jnp.maximum(old, top)
            weight = jnp.exp2((score - wide(top, kn)) * factor)
            part = weight[:, :128]
            for c in range(128, kn, 128):
                part = part + weight[:, c : c + 128]
            mixed = jnp.dot(weight.astype(jnp.bfloat16), v, preferred_element_type=jnp.float32)
            if not own:
                keep = jnp.exp2((old - top) * factor)
                part = part + keep * total[h, span, :]
                mixed = mixed + keep * acc[h, span, :]
            peak[h, span, :] = top
            total[h, span, :] = part
            acc[h, span, :] = mixed
            return carry

        lax.fori_loop(0, heads, one, 0, unroll=4)

    mine_k, mine_v = kv_ref.at[0], kv_ref.at[1]
    attend(mine_k, mine_v, me * tok, 0, half, 0, half, True)
    attend(mine_k, mine_v, me * tok, 0, tok, half, half, True)

    for d in range(1, window + 1):
        @pl.when(me >= d)
        def _(d=d):
            base = (me - d) * tok
            for part in (1, 0):
                block_copy(d, part).wait_recv()
                core_copy(d, part, core).start()
                if d < window:
                    @pl.when(me + 1 < n)
                    def _(part=part):
                        block_copy(d + 1, part).start()
                core_copy(d, part, 1 - core).wait_recv()
                shorter = d == window and part == 0 and 2 * window == n
                attend(
                    buf.at[0, d - 1], buf.at[1, d - 1], base, part * half, half,
                    0, half if shorter else tok, False,
                )
            mask_copy(d).wait_recv()
            chosen = jnp.zeros((PAGE, kvw), jnp.bfloat16)
            for g in range(pages):
                flag = jnp.broadcast_to(mask_rx[d - 1, g : g + 1, :], (PAGE, 128))
                chosen = chosen + wide(flag.astype(jnp.bfloat16), kvw) * buf[
                    core, d - 1, pl.ds(g * PAGE, PAGE), :
                ]
            dec_ref[me - d] = chosen
            for part in (1, 0):
                core_copy(d, part, core).wait_send()

    def finish(h, carry):
        mine = pl.ds(pl.multiple_of(h * 128, 128), 128)
        whole = jnp.sum(total[h], axis=1, keepdims=True)
        out_ref[:, mine] = (acc[h] / whole).astype(jnp.bfloat16)
        return carry

    lax.fori_loop(0, heads, finish, 0)

    for d in range(1, window + 1):
        @pl.when(me + d < n)
        def _(d=d):
            mask_copy(d).wait_send()

        @pl.when((me + 1 < n) & (me >= d - 1))
        def _(d=d):
            for part in (1, 0):
                block_copy(d, part).wait_send()

    for other in range(n):
        @pl.when((other < me) | (other > me + window))
        def _(other=other):
            page_copy(other, me).wait_send()

        @pl.when((other > me) | (other < me - window))
        def _(other=other):
            page_copy(other, other).wait_recv()


def body(queries, keys, values, lengths, page_ranks):
    tok, heads, dim = queries.shape
    kv_heads = keys.shape[1]
    n = lax.axis_size("ctx")
    rep = lax.axis_size("rep")
    window = n // 2
    group = heads * rep // kv_heads
    kvw = kv_heads * dim
    kv = jnp.stack([keys.reshape(tok, kvw), values.reshape(tok, kvw)])
    vmem = pl.BlockSpec(memory_space=pltpu.VMEM)
    smem = pl.BlockSpec(memory_space=pltpu.SMEM)
    flag_rows = -(-(tok // PAGE) // 8) * 8
    dma = pltpu.SemaphoreType.DMA
    context, cache = pl.pallas_call(
        functools.partial(kernel, n, window, heads, group),
        out_shape=(
            jax.ShapeDtypeStruct((tok, heads * dim), jnp.bfloat16),
            jax.ShapeDtypeStruct((n, PAGE, kvw), jnp.bfloat16),
        ),
        in_specs=[smem, smem, vmem, vmem],
        out_specs=(vmem, vmem),
        scratch_shapes=[
            pltpu.VMEM((2, window, tok, kvw), jnp.bfloat16),
            pltpu.VMEM((window, flag_rows, 128), jnp.float32),
            pltpu.VMEM((window, flag_rows, 128), jnp.float32),
            pltpu.VMEM((n, PAGE, kvw), jnp.bfloat16),
            pltpu.VMEM((tok, 128), jnp.int32),
            pltpu.VMEM((heads, tok, 128), jnp.float32),
            pltpu.VMEM((heads, tok, 128), jnp.float32),
            pltpu.VMEM((heads, tok, 128), jnp.float32),
            dma((window, 2)),
            dma((window, 2)),
            dma((window, 2)),
            dma((window, 2)),
            dma((window,)),
            dma((window,)),
            dma((n,)),
            dma((n,)),
        ],
        compiler_params=pltpu.CompilerParams(
            collective_id=0, has_side_effects=True, vmem_limit_bytes=48 * 1024 * 1024
        ),
        cost_estimate=pl.CostEstimate(
            flops=4 * heads * tok * tok * 2 * dim, bytes_accessed=8 * tok * kvw,
            transcendentals=heads * tok * tok * 2,
        ),
    )(lengths, page_ranks, queries.reshape(tok, heads * dim), kv)
    return (
        context.reshape(tok, heads, dim),
        cache.reshape(1, n, PAGE, 1, kv_heads, dim),
    )


def solution(mesh):
    in_specs = (
        P(("groups", "ctx"), ("tp", "rep"), None),
        P(("groups", "ctx"), "tp", None),
        P(("groups", "ctx"), "tp", None),
        P("groups"),
        P(("groups", "ctx")),
    )
    out_specs = (
        P(("groups", "ctx"), ("tp", "rep"), None),
        P(("groups", "ctx"), None, None, "rep", "tp", None),
    )
    return jax.shard_map(body, mesh=mesh, in_specs=in_specs, out_specs=out_specs, check_vma=False)
```

```python
import functools
import math

import jax
import jax.numpy as jnp
from jax import lax
from jax.experimental import pallas as pl
from jax.experimental.pallas import tpu as pltpu
from jax.sharding import PartitionSpec as P

PAGE = 128
MESH = pl.DeviceIdType.MESH
NEG = -1e30


def wide(x, lanes):
    return jnp.concatenate([x] * (lanes // 128), axis=1) if lanes > 128 else x


def kernel(
    n, window, heads, group, lengths, ranks, queries_ref, kv_ref, out_ref, dec_ref,
    q_raw, q_ref, q_sem, buf, mask_tx, mask_rx, stage, start_ref, acc, peak, total,
    z_send, z_recv, c_send, c_recv, m_send, m_recv, p_send, p_recv,
):
    me = lax.axis_index("ctx")
    core = lax.axis_index("rep")
    tok, kvw = kv_ref.shape[1:]
    half = tok // 2
    pages = tok // PAGE
    factor = 128 ** -0.5 * math.log2(math.e)

    fetch = pltpu.make_async_copy(queries_ref, q_raw, q_sem)
    fetch.start()
    barrier = pltpu.get_barrier_semaphore()
    for step in range(1, n):
        pl.semaphore_signal(
            barrier, inc=1, device_id={"ctx": lax.rem(me + step, n)}, device_id_type=MESH
        )
    pl.semaphore_signal(barrier, inc=1, device_id={"rep": 1 - core}, device_id_type=MESH)
    pl.semaphore_wait(barrier, n)

    def rows(part):
        return pl.ds(part * half, half)

    def block_copy(d, part):
        own = kv_ref.at[core, rows(part)]
        return pltpu.make_async_remote_copy(
            src_ref=own if d == 1 else buf.at[core, d - 2, rows(part)],
            dst_ref=buf.at[core, d - 1, rows(part)],
            send_sem=z_send.at[d - 1, part],
            recv_sem=z_recv.at[d - 1, part],
            device_id={"ctx": lax.rem(me + 1, n)},
            device_id_type=MESH,
        )

    def core_copy(d, part, which):
        return pltpu.make_async_remote_copy(
            src_ref=buf.at[which, d - 1, rows(part)],
            dst_ref=buf.at[which, d - 1, rows(part)],
            send_sem=c_send.at[d - 1, part],
            recv_sem=c_recv.at[d - 1, part],
            device_id={"rep": 1 - core},
            device_id_type=MESH,
        )

    def mask_copy(d):
        return pltpu.make_async_remote_copy(
            src_ref=mask_tx.at[d - 1],
            dst_ref=mask_rx.at[d - 1],
            send_sem=m_send.at[d - 1],
            recv_sem=m_recv.at[d - 1],
            device_id={"ctx": lax.rem(me + d, n)},
            device_id_type=MESH,
        )

    def page_copy(there, slot):
        return pltpu.make_async_remote_copy(
            src_ref=stage.at[there],
            dst_ref=dec_ref.at[slot],
            send_sem=p_send.at[there],
            recv_sem=p_recv.at[slot],
            device_id={"ctx": there},
            device_id_type=MESH,
        )

    def page_for(rank):
        page = jnp.zeros((PAGE, kvw), jnp.bfloat16)
        for g in range(pages):
            flag = jnp.where(ranks[g] == rank, jnp.float32(1), jnp.float32(0))
            flag = jnp.full((PAGE, kvw), flag, jnp.float32).astype(jnp.bfloat16)
            page = page + flag * kv_ref[core, pl.ds(g * PAGE, PAGE), :]
        return page

    @pl.when(me + 1 < n)
    def _():
        for part in (1, 0):
            block_copy(1, part).start()

    mask_tx[...] = jnp.zeros_like(mask_tx)

    for there in range(n):
        @pl.when((there < me) | (there > me + window))
        def _(there=there):
            stage[there] = page_for(there)
            page_copy(there, me).start()

    for d in range(1, window + 1):
        @pl.when(me + d < n)
        def _(d=d):
            for g in range(pages):
                chosen = jnp.where(ranks[g] == me + d, jnp.float32(1), jnp.float32(0))
                mask_tx[d - 1, g : g + 1, :] = jnp.full((1, 128), chosen, jnp.float32)
            mask_copy(d).start()

    dec_ref[me] = page_for(me)

    pos = me * tok + lax.broadcasted_iota(jnp.int32, (tok, 128), 0)
    first = jnp.zeros((tok, 128), jnp.int32)
    end = jnp.int32(0)
    for r in range(lengths.shape[0]):
        end = end + lengths[r]
        first = jnp.where(pos >= end, end, first)
    start_ref[...] = first

    def attend(keys_at, values_at, base, k0, kn, q0, qn, own):
        def one(h, carry):
            lane = pl.ds(pl.multiple_of(((core * heads + h) // group) * 128, 128), 128)
            mine = pl.ds(pl.multiple_of(h * 128, 128), 128)
            k = keys_at[pl.ds(k0, kn), lane]
            v = values_at[pl.ds(k0, kn), lane]
            score = lax.dot_general(
                q_ref[pl.ds(q0, qn), mine], k, (((1,), (1,)), ((), ())),
                preferred_element_type=jnp.float32,
            )
            key_pos = base + k0 + lax.broadcasted_iota(jnp.int32, (qn, kn), 1)
            allowed = key_pos >= wide(start_ref[pl.ds(q0, qn), :], kn)
            if own:
                query_pos = base + q0 + lax.broadcasted_iota(jnp.int32, (qn, kn), 0)
                allowed = allowed & (key_pos <= query_pos)
            score = jnp.where(allowed, score, NEG)
            top = jnp.broadcast_to(jnp.max(score, axis=1, keepdims=True), (qn, 128))
            span = pl.ds(q0, qn)
            if not own:
                old = peak[h, span, :]
                top = jnp.maximum(old, top)
            weight = jnp.exp2((score - wide(top, kn)) * factor)
            part = weight[:, :128]
            for c in range(128, kn, 128):
                part = part + weight[:, c : c + 128]
            mixed = jnp.dot(weight.astype(jnp.bfloat16), v, preferred_element_type=jnp.float32)
            if not own:
                keep = jnp.exp2((old - top) * factor)
                part = part + keep * total[h, span, :]
                mixed = mixed + keep * acc[h, span, :]
            peak[h, span, :] = top
            total[h, span, :] = part
            acc[h, span, :] = mixed
            return carry

        lax.fori_loop(0, heads, one, 0, unroll=4)

    fetch.wait()
    for h in range(heads):
        q_ref[:, h * 128 : (h + 1) * 128] = q_raw[:, h, :]

    mine_k, mine_v = kv_ref.at[0], kv_ref.at[1]
    attend(mine_k, mine_v, me * tok, 0, half, 0, half, True)
    attend(mine_k, mine_v, me * tok, 0, tok, half, half, True)

    for d in range(1, window + 1):
        @pl.when(me >= d)
        def _(d=d):
            base = (me - d) * tok
            for part in (1, 0):
                block_copy(d, part).wait_recv()
                core_copy(d, part, core).start()
                if d < window:
                    @pl.when(me + 1 < n)
                    def _(part=part):
                        block_copy(d + 1, part).start()
                core_copy(d, part, 1 - core).wait_recv()
                shorter = d == window and part == 0 and 2 * window == n
                attend(
                    buf.at[0, d - 1], buf.at[1, d - 1], base, part * half, half,
                    0, half if shorter else tok, False,
                )
            mask_copy(d).wait_recv()
            chosen = jnp.zeros((PAGE, kvw), jnp.bfloat16)
            for g in range(pages):
                flag = jnp.broadcast_to(mask_rx[d - 1, g : g + 1, :], (PAGE, 128))
                chosen = chosen + wide(flag.astype(jnp.bfloat16), kvw) * buf[
                    core, d - 1, pl.ds(g * PAGE, PAGE), :
                ]
            dec_ref[me - d] = chosen
            for part in (1, 0):
                core_copy(d, part, core).wait_send()

    def finish(h, carry):
        mine = pl.ds(pl.multiple_of(h * 128, 128), 128)
        whole = jnp.sum(total[h], axis=1, keepdims=True)
        out_ref[:, mine] = (acc[h] / whole).astype(jnp.bfloat16)
        return carry

    lax.fori_loop(0, heads, finish, 0, unroll=2)

    for d in range(1, window + 1):
        @pl.when(me + d < n)
        def _(d=d):
            mask_copy(d).wait_send()

        @pl.when((me + 1 < n) & (me >= d - 1))
        def _(d=d):
            for part in (1, 0):
                block_copy(d, part).wait_send()

    for other in range(n):
        @pl.when((other < me) | (other > me + window))
        def _(other=other):
            page_copy(other, me).wait_send()

        @pl.when((other > me) | (other < me - window))
        def _(other=other):
            page_copy(other, other).wait_recv()


def body(queries, keys, values, lengths, page_ranks):
    tok, heads, dim = queries.shape
    kv_heads = keys.shape[1]
    n = lax.axis_size("ctx")
    rep = lax.axis_size("rep")
    window = n // 2
    group = heads * rep // kv_heads
    kvw = kv_heads * dim
    kv = jnp.stack([keys.reshape(tok, kvw), values.reshape(tok, kvw)])
    vmem = pl.BlockSpec(memory_space=pltpu.VMEM)
    smem = pl.BlockSpec(memory_space=pltpu.SMEM)
    flag_rows = -(-(tok // PAGE) // 8) * 8
    dma = pltpu.SemaphoreType.DMA
    context, cache = pl.pallas_call(
        functools.partial(kernel, n, window, heads, group),
        out_shape=(
            jax.ShapeDtypeStruct((tok, heads * dim), jnp.bfloat16),
            jax.ShapeDtypeStruct((n, PAGE, kvw), jnp.bfloat16),
        ),
        in_specs=[smem, smem, pl.BlockSpec(memory_space=pl.ANY), vmem],
        out_specs=(vmem, vmem),
        scratch_shapes=[
            pltpu.VMEM((tok, heads, dim), jnp.bfloat16),
            pltpu.VMEM((tok, heads * dim), jnp.bfloat16),
            dma,
            pltpu.VMEM((2, window, tok, kvw), jnp.bfloat16),
            pltpu.VMEM((window, flag_rows, 128), jnp.float32),
            pltpu.VMEM((window, flag_rows, 128), jnp.float32),
            pltpu.VMEM((n, PAGE, kvw), jnp.bfloat16),
            pltpu.VMEM((tok, 128), jnp.int32),
            pltpu.VMEM((heads, tok, 128), jnp.float32),
            pltpu.VMEM((heads, tok, 128), jnp.float32),
            pltpu.VMEM((heads, tok, 128), jnp.float32),
            dma((window, 2)),
            dma((window, 2)),
            dma((window, 2)),
            dma((window, 2)),
            dma((window,)),
            dma((window,)),
            dma((n,)),
            dma((n,)),
        ],
        compiler_params=pltpu.CompilerParams(
            collective_id=0, has_side_effects=True, vmem_limit_bytes=48 * 1024 * 1024
        ),
        cost_estimate=pl.CostEstimate(
            flops=4 * heads * tok * tok * 2 * dim, bytes_accessed=8 * tok * kvw,
            transcendentals=heads * tok * tok * 2,
        ),
    )(lengths, page_ranks, queries, kv)
    return (
        context.reshape(tok, heads, dim),
        cache.reshape(1, n, PAGE, 1, kv_heads, dim),
    )


def solution(mesh):
    in_specs = (
        P(("groups", "ctx"), ("tp", "rep"), None),
        P(("groups", "ctx"), "tp", None),
        P(("groups", "ctx"), "tp", None),
        P("groups"),
        P(("groups", "ctx")),
    )
    out_specs = (
        P(("groups", "ctx"), ("tp", "rep"), None),
        P(("groups", "ctx"), None, None, "rep", "tp", None),
    )
    return jax.shard_map(body, mesh=mesh, in_specs=in_specs, out_specs=out_specs, check_vma=False)
```
